32 devices in a mesh: groups: 2 (over x), vel: 16 (over z, y, core).
Axes of the slice: x: 2, y: 2, z: 4, core: 2. Of those that a mesh axis runs over, the one named last changes fastest.
Arguments:
- epoch_maps: bfloat16 [128, 192, 512], P('vel', 'groups'), parts along dimension 1, may hold values from -6 to 6, as said below
- velocity: int32 [16, 2], P('vel'), may hold values from -16 to 16, as said below
- slot_epoch: int32 [64], replicated, may hold values from 0 to 63, each once
- epoch_time: int32 [64], replicated, may hold values from 0 to 127, as said below
Outputs:
- likelihood: float32 [16, 192, 512], P('vel', 'groups'), parts along dimension 1
- best_value: float32 [192, 512], P('groups'), parts along dimension 0
The draws below stay inside these ranges and needn't reach their ends.
There are 2 independent parts, one for each index of `groups`. The reference program is written for one: setup_inputs(seed, part) draws one part's arguments, and reference() takes and returns one part's arrays. A program takes and returns all parts, laid end to end along the dimension named above; an argument that names none is the same for every part. Nothing has to cross between parts.
Inputs may be any that keep to these rules, and one draw needn't show every extreme that they name: `epoch_maps`: the first 64 images are likelihoods, the others weights of at least 0.25 and at most 4. `velocity`: all rows are distinct; rows (16, 16) and (-16, -16) both occur. `epoch_time`: strictly increasing, the first 0 and the last 127. `slot_epoch`: each epoch stands in exactly one slot.
All inputs are finite; a program needn't handle non-finite values.
Results may differ from the reference program's by a relative error of at most 0.0029.
Values may be sent and summed in bfloat16 or wider, within the bound.
No kernel may reach another device: no remote copies, remote signals or barrier semaphores. Data moves between devices by JAX's collectives and lax.ppermute only.
A program may use at most 64 MiB of HBM per device.

```python
import jax
import jax.numpy as jnp
from jax import lax

ROWS = 96
COLS = 512
EPOCHS = 64
VMAX = 16
TMAX = 127
VELS = 16


def draw_epoch_maps(key, part):
    first_key, second_key = jax.random.split(jax.random.fold_in(key, 37), 2)
    map_shape = (EPOCHS, ROWS, COLS)
    likelihoods = jnp.clip(jax.random.normal(first_key, map_shape, jnp.float32), -6.0, 6.0)
    weights = jnp.exp(jax.random.uniform(second_key, map_shape, jnp.float32, jnp.log(0.25), jnp.log(4.0)))
    return jnp.concatenate([likelihoods, weights], axis=0).astype(jnp.bfloat16)


def draw_velocity(key, part):
    first_key, second_key = jax.random.split(jax.random.fold_in(key, 11))
    grid_side = 2 * VMAX + 1
    points = grid_side * grid_side
    shuffled = jax.random.permutation(first_key, points).astype(jnp.int32)
    extreme = (shuffled == 0) | (shuffled == points - 1)
    priority = jnp.where(extreme, (shuffled == points - 1).astype(jnp.int32) - 2, jnp.arange(points, dtype=jnp.int32))
    ranked = shuffled[jnp.argsort(priority)]
    chosen = ranked[:VELS]
    chosen = chosen[jax.random.permutation(second_key, VELS)]
    row_rate = chosen // grid_side - VMAX
    column_rate = chosen % grid_side - VMAX
    return jnp.stack([row_rate, column_rate], axis=1).astype(jnp.int32)


def draw_epoch_time(key, part):
    shuffled = jax.random.permutation(jax.random.fold_in(key, 23), TMAX + 1).astype(jnp.int32)
    extreme = (shuffled == 0) | (shuffled == TMAX)
    priority = jnp.where(extreme, (shuffled == TMAX).astype(jnp.int32) - 2, jnp.arange(TMAX + 1, dtype=jnp.int32))
    ranked = shuffled[jnp.argsort(priority)]
    return jnp.sort(ranked[:EPOCHS]).astype(jnp.int32)


def setup_inputs(seed: int = 0, part: int = 0) -> dict:
    splits = jax.random.split(jax.random.key(seed), 5)
    own_keys = jax.random.split(jax.random.fold_in(splits[4], part), 5)
    return {
        "epoch_maps": draw_epoch_maps(jax.random.fold_in(jax.random.fold_in(splits[4], part), 71), part),
        "velocity": draw_velocity(jax.random.fold_in(splits[4], 71), part),
        "slot_epoch": jax.random.permutation(splits[2], EPOCHS).astype(jnp.int32),
        "epoch_time": draw_epoch_time(jax.random.fold_in(splits[4], 71), part),
    }


SPLINE = [[64.0, 256.0, 64.0, 0.0], [27.0, 235.0, 121.0, 1.0], [8.0, 184.0, 184.0, 8.0], [1.0, 121.0, 235.0, 27.0]]
spline_norm = 147456.0
rate_divisor = 32

def spline_taps(offset):
    whole_shift = offset // 4
    fraction = offset - 4 * whole_shift
    spline_table = jnp.array(SPLINE, dtype=jnp.float32)
    return (whole_shift.astype(jnp.int32), spline_table[fraction])

def shift_axis(epoch_image, whole_shift, weights, margin, axis_number):
    widths = [(0, 0), (0, 0), (0, 0)]
    widths[axis_number] = (margin, margin)
    padded = jnp.pad(epoch_image, widths)
    length = epoch_image.shape[axis_number]
    result = jnp.zeros(epoch_image.shape, jnp.float32)
    for tap_number in range(4):
        position = (margin - 1 + tap_number + whole_shift).astype(jnp.int32)
        result = result + weights[tap_number] * lax.dynamic_slice_in_dim(padded, position, length, axis_number)
    return result

def one_epoch(epoch_image, row_offset, column_offset, margin):
    row_whole, row_weights = spline_taps(row_offset)
    rows_done = shift_axis(epoch_image.astype(jnp.float32), row_whole, row_weights, margin, 1)
    rounded = lax.optimization_barrier(rows_done.astype(jnp.bfloat16))
    column_whole, column_weights = spline_taps(column_offset)
    return shift_axis(rounded.astype(jnp.float32), column_whole, column_weights, margin, 2)

def reference(epoch_maps, velocity, slot_epoch, epoch_time):
    margin = VMAX * TMAX // 128 + 3
    images = jnp.stack([epoch_maps[:EPOCHS], epoch_maps[EPOCHS:]], axis=1)
    slot_time = epoch_time[slot_epoch]

    def per_velocity(rate_pair):
        row_offsets = rate_pair[0] * slot_time // rate_divisor
        column_offsets = rate_pair[1] * slot_time // rate_divisor
        stacks = jax.vmap(one_epoch, in_axes=(0, 0, 0, None))(images, row_offsets, column_offsets, margin)
        stack_sums = lax.optimization_barrier(jnp.sum(stacks, axis=0)) / spline_norm
        return stack_sums[0] / jnp.sqrt(stack_sums[1] + 1.0)
    likelihood = lax.map(per_velocity, velocity)
    return (likelihood, lax.optimization_barrier(jnp.max(likelihood, axis=0)))
```

```python
import functools

import jax
import jax.numpy as jnp
import ml_dtypes
import numpy as np
from jax import lax
from jax.experimental import pallas as pl
from jax.experimental.pallas import tpu as pltpu
from jax.sharding import PartitionSpec as P

SPLINE = np.array(
    [
        [64.0, 256.0, 64.0, 0.0],
        [27.0, 235.0, 121.0, 1.0],
        [8.0, 184.0, 184.0, 8.0],
        [1.0, 121.0, 235.0, 27.0],
    ],
    np.float32,
)
spline_norm = 147456.0
rate_divisor = 32
REACH = 16
HALO = 32
LANES = 128
LINK_SCALE = 64.0


def row_filters(rows, lanes):
    offsets = sorted({(rows * j) % LANES for j in range(max(1, lanes // rows))})
    bands = np.zeros((len(offsets), 2 * LANES, 4 * LANES), np.float32)
    for number, offset in enumerate(offsets):
        for row in range(rows):
            for tap in range(4):
                for fraction in range(4):
                    place = (row - tap + 1) % LANES
                    bands[number, offset + row, fraction * LANES + place] = SPLINE[fraction, tap]
    return offsets, bands.astype(ml_dtypes.bfloat16)


def window_kernel(block, chips, place_ref, image_ref, *refs):
    *window_refs, padded = refs
    columns = image_ref.shape[1]
    padded[:HALO] = jnp.zeros((HALO, padded.shape[1]), padded.dtype)
    padded[HALO + columns :] = jnp.zeros((HALO, padded.shape[1]), padded.dtype)
    for first in range(0, columns, LANES):
        padded[HALO + first : HALO + first + LANES] = image_ref[:, first : first + LANES].T
    for relative, window_ref in enumerate(window_refs):
        chip = place_ref[0] ^ relative
        start = pl.multiple_of(chip * block, block)
        window_ref[...] = padded[pl.ds(start, block + 2 * HALO)]


def stack_kernel(
    block, rows, per_device, epochs, offsets, device_ref, velocity_ref, slot_ref, time_ref, filter_ref, *refs
):
    *window_refs, out_ref, filtered, bins = refs
    hypotheses = velocity_ref.shape[0]
    tall = bins.shape[1]
    bins[...] = jnp.zeros(bins.shape, bins.dtype)
    for relative, window_ref in enumerate(window_refs):
        source = device_ref[0] ^ (2 * relative)
        lanes = window_ref.shape[1]
        for number in range(per_device):
            slot = lax.rem(source * per_device + number, epochs)
            time = time_ref[slot_ref[slot]]
            low = rows * number // LANES * LANES
            high = min(lanes, (rows * (number + 1) + LANES - 1) // LANES * LANES)
            band = filter_ref[offsets.index(rows * number - low), : high - low, :]
            product = jnp.dot(window_ref[:, low:high], band, preferred_element_type=jnp.float32)
            product = product.astype(jnp.bfloat16).astype(jnp.float32)
            for fraction in range(4):
                filtered[fraction] = product[:, fraction * LANES : (fraction + 1) * LANES]

            @pl.loop(0, hypotheses, unroll=min(hypotheses, 16))
            def add(v):
                row_offset = (velocity_ref[v, 0] * time) >> 5
                column_offset = (velocity_ref[v, 1] * time) >> 5
                start = HALO - 1 + (column_offset >> 2)
                shifted = filtered[row_offset & 3, pl.ds(start, tall), :]
                shifted = pltpu.roll(shifted, (LANES - (row_offset >> 2)) & (LANES - 1), 1)
                place = 4 * v + (column_offset & 3)
                bins[place] = bins[place] + shifted

    @pl.loop(0, hypotheses)
    def finish(v):
        total = jnp.zeros((block, LANES), jnp.float32)
        for fraction in range(4):
            for tap in range(4):
                if SPLINE[fraction, tap]:
                    total = total + float(SPLINE[fraction, tap]) * bins[4 * v + fraction, tap : tap + block, :]
        out_ref[v & 1, v >> 1] = (total * (1.0 / spline_norm)).T[:rows]


def assemble_kernel(block, place_ref, *refs):
    *piece_refs, likelihood_ref, best_ref = refs
    for relative, piece_ref in enumerate(piece_refs):
        chip = place_ref[0] ^ relative
        for c in range(len(piece_refs)):

            @pl.when(chip == c)
            def put():
                likelihood_ref[0, :, c * block : (c + 1) * block] = piece_ref[0]
                best_ref[:, c * block : (c + 1) * block] = piece_ref[1]


def local(axis_size, epoch_maps, velocity, slot_epoch, epoch_time):
    per_device, rows, columns = epoch_maps.shape
    epochs = slot_epoch.shape[0]
    half = axis_size // 2
    chips = half // 2
    block = columns // chips
    device = lax.axis_index("vel").astype(jnp.int32)
    place = (device % half // 2).reshape(1)

    def swap(array, bits):
        return lax.ppermute(array, "vel", [(i, i ^ bits) for i in range(axis_size)])

    smem = pl.BlockSpec(memory_space=pltpu.SMEM)
    vmem = pl.BlockSpec(memory_space=pltpu.VMEM)
    lanes = per_device * rows
    wide = block + 2 * HALO
    windows = pl.pallas_call(
        functools.partial(window_kernel, block, chips),
        out_shape=[jax.ShapeDtypeStruct((wide, lanes), epoch_maps.dtype)] * chips,
        in_specs=[smem, vmem],
        out_specs=[vmem] * chips,
        scratch_shapes=[pltpu.VMEM((columns + 2 * HALO, lanes), epoch_maps.dtype)],
        name="windows",
    )(place, epoch_maps.reshape(lanes, columns))
    windows = [windows[0]] + [swap(windows[x], 2 * x) for x in range(1, chips)]

    rates = jnp.concatenate([velocity, swap(velocity, 1)])
    rates = jnp.concatenate([rates] + [swap(rates, 2 * x) for x in range(1, chips)])
    rates = jnp.concatenate([rates, swap(rates, half)])

    offsets, bands = row_filters(rows, lanes)
    tall = (block + 3 + 7) // 8 * 8
    partial = pl.pallas_call(
        functools.partial(stack_kernel, block, rows, per_device, epochs, offsets),
        out_shape=jax.ShapeDtypeStruct((2, half, rows, block), jnp.float32),
        in_specs=[smem] * 4 + [vmem] * (1 + chips),
        out_specs=vmem,
        scratch_shapes=[
            pltpu.VMEM((4, wide, LANES), jnp.float32),
            pltpu.VMEM((4 * axis_size, tall, LANES), jnp.float32),
        ],
        compiler_params=pltpu.CompilerParams(vmem_limit_bytes=48 * 1024 * 1024),
        name="stack",
    )(device.reshape(1), rates, slot_epoch, epoch_time, jnp.asarray(bands), *windows)

    own = ((partial[0] + swap(partial[1], 1)) * LINK_SCALE).astype(jnp.float16)
    other = swap(own, half)
    other = jnp.concatenate([other[chips:], other[:chips]])
    own = own.astype(jnp.float32) * (1.0 / LINK_SCALE)
    other = other.astype(jnp.float32) * (1.0 / LINK_SCALE)
    first = device < half
    sums = jnp.where(first, own, other)
    weights = jnp.where(first, other, own)
    likelihood = sums / jnp.sqrt(weights + 1.0)
    best = jnp.max(likelihood, axis=0)
    best = jnp.maximum(best, swap(best, 1))
    pieces = [jnp.stack([likelihood[x], best]) for x in range(chips)]
    pieces = [pieces[0]] + [swap(pieces[x], 2 * x) for x in range(1, chips)]
    return pl.pallas_call(
        functools.partial(assemble_kernel, block),
        out_shape=[
            jax.ShapeDtypeStruct((1, rows, columns), jnp.float32),
            jax.ShapeDtypeStruct((rows, columns), jnp.float32),
        ],
        in_specs=[smem] + [vmem] * chips,
        out_specs=[vmem] * 2,
        name="assemble",
    )(place, *pieces)


def solution(mesh):
    return jax.shard_map(
        functools.partial(local, mesh.shape["vel"]),
        mesh=mesh,
        in_specs=(P("vel", "groups", None), P("vel", None), P(), P()),
        out_specs=(P("vel", "groups", None), P("groups", None)),
        check_vma=False,
    )
```

```python
import functools

import jax
import jax.numpy as jnp
import ml_dtypes
import numpy as np
from jax import lax
from jax.experimental import pallas as pl
from jax.experimental.pallas import tpu as pltpu
from jax.sharding import PartitionSpec as P

SPLINE = np.array(
    [
        [64.0, 256.0, 64.0, 0.0],
        [27.0, 235.0, 121.0, 1.0],
        [8.0, 184.0, 184.0, 8.0],
        [1.0, 121.0, 235.0, 27.0],
    ],
    np.float32,
)
spline_norm = 147456.0
rate_divisor = 32
HALO = 24
LANES = 128
PACK = 16
LINK_SCALE = 64.0


def row_filter(rows):
    band = np.zeros((rows, 4 * LANES), np.float32)
    for row in range(rows):
        for tap in range(4):
            for fraction in range(4):
                band[row, fraction * LANES + (row - tap + 1) % LANES] = SPLINE[fraction, tap]
    return band.astype(ml_dtypes.bfloat16)


def window_kernel(block, chips, place_ref, image_ref, *refs):
    *window_refs, padded = refs
    lanes, columns = image_ref.shape
    image = jnp.concatenate([image_ref[...], jnp.zeros((lanes, LANES), image_ref.dtype)], axis=1)
    image = pltpu.roll(image, HALO, 1)
    for first in range(0, columns + LANES, LANES):
        padded[first : first + LANES] = image[:, first : first + LANES].T
    for relative, window_ref in enumerate(window_refs):
        start = pl.multiple_of((place_ref[0] ^ relative) * block, block)
        window_ref[...] = padded[pl.ds(start, block + 2 * HALO)]


def stack_kernel(block, rows, sources, images, first, scale, carried, time_ref, rate_ref, filter_ref, *refs):
    window_refs, before, refs = refs[: len(sources)], refs[len(sources) :][:carried], refs[len(sources) + carried :]
    keep_ref, send_ref, bands, filtered, *bins = refs
    lanes = window_refs[0].shape[1]
    together = len(bins)
    turns = bins[0].shape[0] // 4
    reach = bins[0].shape[1] - PACK
    wide = window_refs[0].shape[0]
    offsets = sorted({rows * number % LANES for number in range(images)})
    bands[...] = jnp.zeros(bands.shape, bands.dtype)
    for number, offset in enumerate(offsets):
        bands[number, offset : offset + rows] = filter_ref[...]
    for part in bins:
        part[...] = jnp.zeros(part.shape, part.dtype)
    if filtered.shape[2] > wide:
        filtered[:, :, wide:] = jnp.zeros((*filtered.shape[:2], filtered.shape[2] - wide, LANES), filtered.dtype)
    for index, (relative, window_ref) in enumerate(zip(sources, window_refs)):
        for number in range(images):
            time = time_ref[relative * images + number]
            held = index * images + number
            low = rows * number // LANES * LANES
            high = min(lanes, (rows * (number + 1) + LANES - 1) // LANES * LANES)
            band = bands[offsets.index(rows * number - low), : high - low]
            product = jnp.dot(window_ref[:, low:high], band, preferred_element_type=jnp.float32)
            product = product.astype(jnp.bfloat16)
            for fraction in range(4):
                filtered[held, fraction, :wide] = product[:, fraction * LANES : (fraction + 1) * LANES]

            def add(turn, _, time=time, held=held):
                for lane in range(together):
                    v = first + turn * together + lane
                    row_offset = (rate_ref[v, 0] * time) >> 5
                    column_offset = (rate_ref[v, 1] * time) >> 5
                    start = HALO - 1 + (column_offset >> 2)
                    even = pl.multiple_of((start >> 4) << 4, PACK)
                    shifted = filtered[held, row_offset & 3, pl.ds(even, reach), :]
                    shifted = pltpu.roll(shifted, (LANES - (row_offset >> 2)) & (LANES - 1), 1)
                    place = 4 * turn + (column_offset & 3)
                    bins[lane][place, pl.ds(PACK - (start - even), reach), :] += shifted.astype(jnp.float32)
                return _

            if turns == 1:
                add(0, 0)
            else:
                lax.fori_loop(0, turns, add, 0)

    def finish(turn, _):
        for lane in range(together):
            v = turn * together + lane
            total = jnp.zeros((block, LANES), jnp.float32)
            for fraction in range(4):
                for tap in range(4):
                    if SPLINE[fraction, tap]:
                        taken = bins[lane][4 * turn + fraction, PACK + tap : PACK + tap + block, :]
                        total = total + float(SPLINE[fraction, tap]) * taken
            total = (total * scale).T[:rows]
            if before:
                total = total + before[lane & 1][v >> 1]
            (send_ref if lane & 1 else keep_ref)[v >> 1] = total
        return _

    if turns == 1:
        finish(0, 0)
    else:
        lax.fori_loop(0, turns, finish, 0)


def arrange(pieces, place):
    step = 1
    while step < len(pieces):
        flip = (place & step) != 0
        pieces = [jnp.where(flip, pieces[x ^ step], pieces[x]) for x in range(len(pieces))]
        step *= 2
    return jnp.concatenate(pieces, axis=-1)


def local(axis_size, epoch_maps, velocity, slot_epoch, epoch_time):
    per_device, rows, columns = epoch_maps.shape
    epochs = slot_epoch.shape[0]
    half = axis_size // 2
    chips = half // 2
    block = columns // chips
    device = lax.axis_index("vel").astype(jnp.int32)
    place = device % half // 2

    def swap(array, bits):
        return lax.ppermute(array, "vel", [(i, i ^ bits) for i in range(axis_size)])

    smem = pl.BlockSpec(memory_space=pltpu.SMEM)
    vmem = pl.BlockSpec(memory_space=pltpu.VMEM)
    lanes = per_device * rows
    wide = block + 2 * HALO
    shape = jax.ShapeDtypeStruct

    windows = pl.pallas_call(
        functools.partial(window_kernel, block, chips),
        out_shape=[shape((wide, lanes), epoch_maps.dtype)] * chips,
        in_specs=[smem, vmem],
        out_specs=[vmem] * chips,
        scratch_shapes=[pltpu.VMEM((columns + LANES, lanes), epoch_maps.dtype)],
        name="windows",
    )(place.reshape(1), epoch_maps.reshape(lanes, columns))

    rates = jnp.concatenate([velocity] + [swap(velocity, 2 * x) for x in range(1, chips)])
    windows, rates = lax.optimization_barrier((windows, rates))
    rates = jnp.concatenate([rates, swap(rates, half)])
    rates = jnp.stack([rates, swap(rates, 1)], axis=1).reshape(axis_size, 2)
    windows = [windows[0]] + [swap(windows[x], 2 * x) for x in range(1, chips)]

    source = device ^ (2 * jnp.arange(chips, dtype=jnp.int32))
    slot = (source[:, None] * per_device + jnp.arange(per_device, dtype=jnp.int32)) % epochs
    every = jnp.arange(epochs, dtype=jnp.int32)
    epoch = jnp.sum(jnp.where(slot[..., None] == every, slot_epoch, 0), axis=-1)
    times = jnp.sum(jnp.where(epoch[..., None] == every, epoch_time, 0), axis=-1).reshape(-1)

    reach = (block + 2 + PACK + PACK - 1) // PACK * PACK
    band = jnp.asarray(row_filter(rows))

    def stack(sources, first, count, carried=()):
        together = min(count, 16)
        tall = max(wide, 2 * PACK + reach)
        return pl.pallas_call(
            functools.partial(
                stack_kernel, block, rows, sources, per_device, first, LINK_SCALE / spline_norm, len(carried)
            ),
            out_shape=[shape((count // 2, rows, block), jnp.float32)] * 2,
            in_specs=[smem] * 2 + [vmem] * (1 + len(sources) + len(carried)),
            out_specs=[vmem] * 2,
            scratch_shapes=[
                pltpu.VMEM((4, 2 * LANES, 4 * LANES), jnp.bfloat16),
                pltpu.VMEM((len(sources) * per_device, 4, tall, LANES), jnp.bfloat16),
            ]
            + [pltpu.VMEM((4 * count // together, reach + PACK, LANES), jnp.float32)] * together,
            compiler_params=pltpu.CompilerParams(vmem_limit_bytes=40 * 1024 * 1024),
            name="stack",
        )(times, rates, band, *[windows[x] for x in sources], *carried)

    late = [chips - 1]
    early = [x for x in range(1, chips) if x not in late]
    keep, send = stack([0], 0, axis_size)
    if early:
        keep, send = stack(early, 0, axis_size, (keep, send))
    keep_far, send_far = stack(late, half, half, (keep[chips:], send[chips:]))
    far = (keep_far + swap(send_far, 1)).astype(jnp.float16)
    near = (keep[:chips], send[:chips])
    far, near = lax.optimization_barrier((far, near))
    other = swap(far, half).astype(jnp.float32) * (1.0 / LINK_SCALE)
    keep_near, send_near = stack(late, 0, half, near)
    near = (keep_near + swap(send_near, 1)) * (1.0 / LINK_SCALE)
    first = device < half
    near = jnp.where(first, near, other) / jnp.sqrt(jnp.where(first, other, near) + 1.0)
    best = jnp.max(near, axis=0)
    best = jnp.maximum(jnp.maximum(best, swap(best, 1)), jnp.maximum(swap(best, half), swap(best, half + 1)))

    pieces = [(jnp.concatenate([near[x], best]) * LINK_SCALE).astype(jnp.float16) for x in range(chips)]
    pieces = [pieces[0]] + [swap(pieces[x], 2 * x) for x in range(1, chips)]
    whole = arrange(pieces, place).astype(jnp.float32) * (1.0 / LINK_SCALE)
    return whole[None, :rows], whole[rows:]


def solution(mesh):
    return jax.shard_map(
        functools.partial(local, mesh.shape["vel"]),
        mesh=mesh,
        in_specs=(P("vel", "groups", None), P("vel", None), P(), P()),
        out_specs=(P("vel", "groups", None), P("groups", None)),
        check_vma=False,
    )
```

```python
import functools

import jax
import jax.numpy as jnp
import ml_dtypes
import numpy as np
from jax import lax
from jax.experimental import pallas as pl
from jax.experimental.pallas import tpu as pltpu
from jax.sharding import PartitionSpec as P

SPLINE = np.array(
    [
        [64.0, 256.0, 64.0, 0.0],
        [27.0, 235.0, 121.0, 1.0],
        [8.0, 184.0, 184.0, 8.0],
        [1.0, 121.0, 235.0, 27.0],
    ],
    np.float32,
)
spline_norm = 147456.0
rate_divisor = 32
HALO = 24
LANES = 128
PACK = 16
LINK_SCALE = 64.0


def row_filter(rows):
    band = np.zeros((rows, 4 * LANES), np.float32)
    for row in range(rows):
        for tap in range(4):
            for fraction in range(4):
                band[row, fraction * LANES + (row - tap + 1) % LANES] = SPLINE[fraction, tap]
    return band.astype(ml_dtypes.bfloat16)


def window_kernel(block, per_device, device_ref, slot_ref, epoch_time_ref, image_ref, time_ref, *refs):
    *window_refs, padded = refs
    chips = len(window_refs)
    epochs = slot_ref.shape[0]
    place = (device_ref[0] >> 1) & (chips - 1)
    for relative in range(chips):
        source = device_ref[0] ^ (2 * relative)
        for number in range(per_device):
            slot = lax.rem(source * per_device + number, epochs)
            time_ref[relative * per_device + number] = epoch_time_ref[slot_ref[slot]]
    lanes, columns = image_ref.shape
    image = jnp.concatenate([image_ref[...], jnp.zeros((lanes, LANES), image_ref.dtype)], axis=1)
    image = pltpu.roll(image, HALO, 1)
    for first in range(0, columns + LANES, LANES):
        padded[first : first + LANES] = image[:, first : first + LANES].T
    for relative, window_ref in enumerate(window_refs):
        start = pl.multiple_of((place ^ relative) * block, block)
        window_ref[...] = padded[pl.ds(start, block + 2 * HALO)]


def stack_kernel(block, rows, sources, images, first, scale, fresh, carried, time_ref, rate_ref, filter_ref, *refs):
    count = len(sources)
    given, before, refs = refs[:count], refs[count:][:carried], refs[count + carried :]
    keep_ref, send_ref, *refs = refs
    kept, refs = (refs[:count], refs[count:]) if fresh else (given, refs)
    bands, own, times, rates, semaphores, *bins = refs
    fetches = [
        pltpu.make_async_copy(time_ref, times, semaphores.at[0]),
        pltpu.make_async_copy(rate_ref, rates, semaphores.at[1]),
    ]
    for fetch in fetches:
        fetch.start()
    if fresh and sources[0] == 0:
        copy = pltpu.make_async_copy(given[0], own, semaphores.at[2])
        copy.start()
    together = len(bins)
    turns = bins[0].shape[0] // 4
    reach = bins[0].shape[1] - PACK
    wide = block + 2 * HALO
    lanes = images * rows
    offsets = sorted({rows * number % LANES for number in range(images)})
    if fresh:
        bands[...] = jnp.zeros(bands.shape, bands.dtype)
        for number, offset in enumerate(offsets):
            bands[number, offset : offset + rows] = filter_ref[...]
        for filtered in kept:
            if filtered.shape[2] > wide:
                filtered[:, :, wide:] = jnp.zeros((*filtered.shape[:2], filtered.shape[2] - wide, LANES), filtered.dtype)
    for part in bins:
        part[...] = jnp.zeros(part.shape, part.dtype)
    for index, relative in enumerate(sources):
        filtered, window_ref = kept[index], given[index]
        if fresh and relative == 0:
            copy.wait()
            window_ref = own
        for number in range(images):
            if fresh:
                low = rows * number // LANES * LANES
                high = min(lanes, (rows * (number + 1) + LANES - 1) // LANES * LANES)
                band = bands[offsets.index(rows * number - low), : high - low]
                product = jnp.dot(window_ref[:, low:high], band, preferred_element_type=jnp.float32)
                product = product.astype(jnp.bfloat16)
                for fraction in range(4):
                    filtered[number, fraction, :wide] = product[:, fraction * LANES : (fraction + 1) * LANES]
            if index == 0 and number == 0:
                for fetch in fetches:
                    fetch.wait()
            time = times[relative * images + number]

            def add(turn, _, time=time, number=number, filtered=filtered):
                for lane in range(together):
                    v = first + turn * together + lane
                    rate = (v & 1) * (rates.shape[0] // 2) + (v >> 1) * 2
                    row_offset = (rates[rate] * time) >> 5
                    column_offset = (rates[rate + 1] * time) >> 5
                    start = HALO - 1 + (column_offset >> 2)
                    even = pl.multiple_of((start >> 4) << 4, PACK)
                    shifted = filtered[number, row_offset & 3, pl.ds(even, reach), :]
                    shifted = pltpu.roll(shifted, (LANES - (row_offset >> 2)) & (LANES - 1), 1)
                    place = 4 * turn + (column_offset & 3)
                    bins[lane][place, pl.ds(PACK - (start - even), reach), :] += shifted.astype(jnp.float32)
                return _

            if turns == 1:
                add(0, 0)
            else:
                lax.fori_loop(0, turns, add, 0)

    def finish(turn, _):
        for lane in range(together):
            v = turn * together + lane
            total = jnp.zeros((block, LANES), jnp.float32)
            for fraction in range(4):
                for tap in range(4):
                    if SPLINE[fraction, tap]:
                        taken = bins[lane][4 * turn + fraction, PACK + tap : PACK + tap + block, :]
                        total = total + float(SPLINE[fraction, tap]) * taken
            total = (total * scale).T[:rows]
            if before:
                total = total + before[lane & 1][v >> 1]
            (send_ref if lane & 1 else keep_ref)[v >> 1] = total
        return _

    if turns == 1:
        finish(0, 0)
    else:
        lax.fori_loop(0, turns, finish, 0)


def arrange(pieces, place):
    step = 1
    while step < len(pieces):
        flip = (place & step) != 0
        pieces = [jnp.where(flip, pieces[x ^ step], pieces[x]) for x in range(len(pieces))]
        step *= 2
    return jnp.concatenate(pieces, axis=-1)


def local(axis_size, epoch_maps, velocity, slot_epoch, epoch_time):
    per_device, rows, columns = epoch_maps.shape
    epochs = slot_epoch.shape[0]
    half = axis_size // 2
    chips = half // 2
    block = columns // chips
    device = lax.axis_index("vel").astype(jnp.int32)
    place = device % half // 2

    def swap(array, bits):
        return lax.ppermute(array, "vel", [(i, i ^ bits) for i in range(axis_size)])

    smem = pl.BlockSpec(memory_space=pltpu.SMEM)
    vmem = pl.BlockSpec(memory_space=pltpu.VMEM)
    hbm = pl.BlockSpec(memory_space=pltpu.HBM)
    lanes = per_device * rows
    wide = block + 2 * HALO
    shape = jax.ShapeDtypeStruct

    def cost(microseconds):
        return pl.CostEstimate(flops=microseconds * 10**9, bytes_accessed=microseconds * 3 * 10**6, transcendentals=0)


    rates = velocity.reshape(-1)
    rates = jnp.concatenate([rates] + [swap(rates, 2 * x) for x in range(1, chips)])
    times, *windows = pl.pallas_call(
        functools.partial(window_kernel, block, per_device),
        out_shape=[shape((chips * per_device,), jnp.int32)] + [shape((wide, lanes), epoch_maps.dtype)] * chips,
        in_specs=[smem] * 3 + [vmem],
        out_specs=[smem] + [vmem] * chips,
        scratch_shapes=[pltpu.VMEM((columns + LANES, lanes), epoch_maps.dtype)],
        compiler_params=pltpu.CompilerParams(vmem_limit_bytes=16 * 1024 * 1024),
        cost_estimate=cost(3),
        name="windows",
    )(device.reshape(1), slot_epoch, epoch_time, epoch_maps.reshape(lanes, columns))

    windows[2:], rates = lax.optimization_barrier((windows[2:], rates))
    rates = jnp.concatenate([rates, swap(rates, half)])
    rates = jnp.concatenate([rates, swap(rates, 1)])
    windows = [windows[0]] + [swap(windows[x], 2 * x) for x in range(1, chips)]

    reach = (block + 2 + PACK + PACK - 1) // PACK * PACK
    band = jnp.asarray(row_filter(rows))

    tall = max(wide, 2 * PACK + reach)

    def stack(sources, first, count, given, carried=(), fresh=True):
        together = min(count, 16)
        filtered = shape((per_device, 4, tall, LANES), jnp.bfloat16)
        keep, send, *filtered = pl.pallas_call(
            functools.partial(
                stack_kernel,
                *(block, rows, sources, per_device, first, LINK_SCALE / spline_norm, fresh, len(carried)),
            ),
            out_shape=[shape((count // 2, rows, block), jnp.float32)] * 2 + [filtered] * (fresh * len(sources)),
            in_specs=[hbm, hbm, vmem]
            + [hbm if x == 0 and fresh else vmem for x in sources]
            + [vmem] * len(carried),
            out_specs=[vmem] * (2 + fresh * len(sources)),
            scratch_shapes=[
                pltpu.VMEM((4, 2 * LANES, 4 * LANES), jnp.bfloat16),
                pltpu.VMEM((wide, lanes), jnp.bfloat16),
                pltpu.SMEM(times.shape, jnp.int32),
                pltpu.SMEM(rates.shape, jnp.int32),
                pltpu.SemaphoreType.DMA((3,)),
            ]
            + [pltpu.VMEM((4 * count // together, reach + PACK, LANES), jnp.float32)] * together,
            compiler_params=pltpu.CompilerParams(vmem_limit_bytes=32 * 1024 * 1024),
            cost_estimate=cost(5),
            name="stack",
        )(times, rates, band, *given, *carried)
        return keep, send, filtered

    late = [chips - 1]
    early = [x for x in range(1, chips) if x not in late]
    keep, send, _ = stack([0], 0, axis_size, windows[:1])
    far, early_rows = (keep[chips:], send[chips:]), []
    if early:
        *far, early_rows = stack(early, half, half, [windows[x] for x in early], far)
    keep_far, send_far, late_rows = stack(late, half, half, [windows[x] for x in late], far)
    far = keep_far + swap(send_far.astype(jnp.float16), 1).astype(jnp.float32)
    far = far.astype(jnp.float16)
    far, near = lax.optimization_barrier((far, (keep[:chips], send[:chips])))
    other = swap(far, half).astype(jnp.float32) * (1.0 / LINK_SCALE)
    keep_near, send_near, _ = stack(early + late, 0, half, early_rows + late_rows, near, fresh=False)
    send_near, other = lax.optimization_barrier((send_near.astype(jnp.float16), other))
    near = (keep_near + swap(send_near, 1).astype(jnp.float32)) * (1.0 / LINK_SCALE)
    first = device < half
    near = jnp.where(first, near, other) / jnp.sqrt(jnp.where(first, other, near) + 1.0)
    near = (near * LINK_SCALE).astype(jnp.float16)
    best = jnp.max(near, axis=0)
    best = jnp.maximum(jnp.maximum(best, swap(best, 1)), jnp.maximum(swap(best, half), swap(best, half + 1)))

    pieces = [jnp.concatenate([near[x], best]) for x in range(chips)]
    pieces = [pieces[0]] + [swap(pieces[x], 2 * x) for x in range(1, chips)]
    whole = arrange(pieces, place).astype(jnp.float32) * (1.0 / LINK_SCALE)
    return whole[None, :rows], whole[rows:]


def solution(mesh):
    return jax.shard_map(
        functools.partial(local, mesh.shape["vel"]),
        mesh=mesh,
        in_specs=(P("vel", "groups", None), P("vel", None), P(), P()),
        out_specs=(P("vel", "groups", None), P("groups", None)),
        check_vma=False,
    )
```

```python
import functools

import jax
import jax.numpy as jnp
import ml_dtypes
import numpy as np
from jax import lax
from jax.experimental import pallas as pl
from jax.experimental.pallas import tpu as pltpu
from jax.sharding import PartitionSpec as P

SPLINE = np.array(
    [
        [64.0, 256.0, 64.0, 0.0],
        [27.0, 235.0, 121.0, 1.0],
        [8.0, 184.0, 184.0, 8.0],
        [1.0, 121.0, 235.0, 27.0],
    ],
    np.float32,
)
spline_norm = 147456.0
HALO = 24
LANES = 128
PACK = 16
LINK_SCALE = 64.0


def row_filter(rows):
    band = np.zeros((rows, 4 * LANES), np.float32)
    for row in range(rows):
        for tap in range(4):
            for fraction in range(4):
                band[row, fraction * LANES + (row - tap + 1) % LANES] = SPLINE[fraction, tap]
    return band.astype(ml_dtypes.bfloat16)


def window_kernel(block, image_ref, *refs):
    *window_refs, padded = refs
    place = (lax.axis_index("vel") >> 1) & (len(window_refs) - 1)
    lanes, columns = image_ref.shape
    image = jnp.concatenate([image_ref[...], jnp.zeros((lanes, LANES), image_ref.dtype)], axis=1)
    image = pltpu.roll(image, HALO, 1)
    for first in range(0, columns + LANES, LANES):
        padded[first : first + LANES] = image[:, first : first + LANES].T
    for relative, window_ref in enumerate(window_refs):
        start = pl.multiple_of((place ^ relative) * block, block)
        window_ref[...] = padded[pl.ds(start, block + 2 * HALO)]


def stack_kernel(block, rows, sources, images, first, scale, fresh, carried, slot_ref, time_ref, rate_ref, filter_ref, *refs):
    count = len(sources)
    given, before, refs = refs[:count], refs[count:][:carried], refs[count + carried :]
    keep_ref, send_ref, *refs = refs
    kept, refs = (refs[:count], refs[count:]) if fresh else (given, refs)
    bands, own, slots, times, rates, semaphores, *bins = refs
    fetches = [
        pltpu.make_async_copy(slot_ref, slots, semaphores.at[0]),
        pltpu.make_async_copy(time_ref, times, semaphores.at[1]),
        pltpu.make_async_copy(rate_ref, rates, semaphores.at[2]),
    ]
    for fetch in fetches:
        fetch.start()
    if fresh and sources[0] == 0:
        copy = pltpu.make_async_copy(given[0], own, semaphores.at[3])
        copy.start()
    chips = rates.shape[0] // 8
    together = len(bins)
    turns = bins[0].shape[0] // 4
    reach = bins[0].shape[1] - PACK
    wide = block + 2 * HALO
    lanes = images * rows
    offsets = sorted({rows * number % LANES for number in range(images)})
    if fresh:
        bands[...] = jnp.zeros(bands.shape, bands.dtype)
        for number, offset in enumerate(offsets):
            bands[number, offset : offset + rows] = filter_ref[...]
        for filtered in kept:
            if filtered.shape[2] > wide:
                filtered[:, :, wide:] = jnp.zeros((*filtered.shape[:2], filtered.shape[2] - wide, LANES), filtered.dtype)
    for part in bins:
        part[...] = jnp.zeros(part.shape, part.dtype)
    for index, relative in enumerate(sources):
        filtered, window_ref = kept[index], given[index]
        if fresh and relative == 0:
            copy.wait()
            window_ref = own
        for number in range(images):
            if fresh:
                low = rows * number // LANES * LANES
                high = min(lanes, (rows * (number + 1) + LANES - 1) // LANES * LANES)
                band = bands[offsets.index(rows * number - low), : high - low]
                product = jnp.dot(window_ref[:, low:high], band, preferred_element_type=jnp.float32)
                product = product.astype(jnp.bfloat16)
                for fraction in range(4):
                    filtered[number, fraction, :wide] = product[:, fraction * LANES : (fraction + 1) * LANES]
            if index == 0 and number == 0:
                for fetch in fetches:
                    fetch.wait()
            source = lax.axis_index("vel") ^ (2 * relative)
            time = times[slots[lax.rem(source * images + number, times.shape[0])]]

            def add(turn, _, time=time, number=number, filtered=filtered):
                for lane in range(together):
                    v = first + turn * together + lane
                    rate = (v >> 1) // chips * 4 * chips + (v & 1) * 2 * chips + (v >> 1) % chips * 2
                    row_offset = (rates[rate] * time) >> 5
                    column_offset = (rates[rate + 1] * time) >> 5
                    start = HALO - 1 + (column_offset >> 2)
                    even = pl.multiple_of((start >> 4) << 4, PACK)
                    shifted = filtered[number, row_offset & 3, pl.ds(even, reach), :]
                    shifted = pltpu.roll(shifted, (LANES - (row_offset >> 2)) & (LANES - 1), 1)
                    place = 4 * turn + (column_offset & 3)
                    bins[lane][place, pl.ds(PACK - (start - even), reach), :] += shifted.astype(jnp.float32)
                return _

            if turns == 1:
                add(0, 0)
            else:
                lax.fori_loop(0, turns, add, 0)

    def finish(turn, _):
        for lane in range(together):
            v = turn * together + lane
            total = jnp.zeros((block, LANES), jnp.float32)
            for fraction in range(4):
                for tap in range(4):
                    if SPLINE[fraction, tap]:
                        taken = bins[lane][4 * turn + fraction, PACK + tap : PACK + tap + block, :]
                        total = total + float(SPLINE[fraction, tap]) * taken
            total = (total * scale).T[:rows]
            if before:
                total = total + before[lane & 1][v >> 1]
            (send_ref if lane & 1 else keep_ref)[v >> 1] = total
        return _

    if turns == 1:
        finish(0, 0)
    else:
        lax.fori_loop(0, turns, finish, 0)


def arrange(pieces, place):
    step = 1
    while step < len(pieces):
        flip = (place & step) != 0
        pieces = [jnp.where(flip, pieces[x ^ step], pieces[x]) for x in range(len(pieces))]
        step *= 2
    return jnp.concatenate(pieces, axis=-1)


def local(axis_size, epoch_maps, velocity, slot_epoch, epoch_time):
    per_device, rows, columns = epoch_maps.shape
    half = axis_size // 2
    chips = half // 2
    block = columns // chips
    device = lax.axis_index("vel").astype(jnp.int32)
    place = device % half // 2

    def swap(array, bits):
        return lax.ppermute(array, "vel", [(i, i ^ bits) for i in range(axis_size)])

    smem = pl.BlockSpec(memory_space=pltpu.SMEM)
    vmem = pl.BlockSpec(memory_space=pltpu.VMEM)
    hbm = pl.BlockSpec(memory_space=pltpu.HBM)
    lanes = per_device * rows
    wide = block + 2 * HALO
    shape = jax.ShapeDtypeStruct

    def cost(microseconds):
        return pl.CostEstimate(flops=microseconds * 10**9, bytes_accessed=microseconds * 3 * 10**6, transcendentals=0)


    rates = velocity.reshape(-1)
    rates = jnp.concatenate([rates] + [swap(rates, 2 * x) for x in range(1, chips)])
    windows = list(pl.pallas_call(
        functools.partial(window_kernel, block),
        out_shape=[shape((wide, lanes), epoch_maps.dtype)] * chips,
        in_specs=[vmem],
        out_specs=[vmem] * chips,
        scratch_shapes=[pltpu.VMEM((columns + LANES, lanes), epoch_maps.dtype)],
        compiler_params=pltpu.CompilerParams(vmem_limit_bytes=56 * 1024 * 1024),
        cost_estimate=cost(3),
        name="windows",
    )(epoch_maps.reshape(lanes, columns)))
    late = [chips - 1]
    windows[2:], rates = lax.optimization_barrier((windows[2:], rates))
    rates = jnp.concatenate([rates, swap(rates, 1)])
    rates = jnp.concatenate([rates, swap(rates, half)])
    windows = [windows[0]] + [swap(windows[x], 2 * x) for x in range(1, chips)]

    reach = (block + 2 + PACK + PACK - 1) // PACK * PACK
    band = jnp.asarray(row_filter(rows))

    tall = max(wide, 2 * PACK + reach)

    def stack(sources, first, count, given, carried=(), fresh=True):
        together = min(count, 16)
        filtered = shape((per_device, 4, tall, LANES), jnp.bfloat16)
        keep, send, *filtered = pl.pallas_call(
            functools.partial(
                stack_kernel,
                *(block, rows, sources, per_device, first, LINK_SCALE / spline_norm, fresh, len(carried)),
            ),
            out_shape=[shape((count // 2, rows, block), jnp.float32)] * 2 + [filtered] * (fresh * len(sources)),
            in_specs=[hbm, hbm, hbm, vmem]
            + [hbm if x == 0 and fresh else vmem for x in sources]
            + [vmem] * len(carried),
            out_specs=[vmem] * (2 + fresh * len(sources)),
            scratch_shapes=[
                pltpu.VMEM((4, 2 * LANES, 4 * LANES), jnp.bfloat16),
                pltpu.VMEM((wide, lanes), jnp.bfloat16),
                pltpu.SMEM(slot_epoch.shape, jnp.int32),
                pltpu.SMEM(epoch_time.shape, jnp.int32),
                pltpu.SMEM(rates.shape, jnp.int32),
                pltpu.SemaphoreType.DMA((4,)),
            ]
            + [pltpu.VMEM((4 * count // together, reach + PACK, LANES), jnp.float32)] * together,
            compiler_params=pltpu.CompilerParams(vmem_limit_bytes=32 * 1024 * 1024),
            cost_estimate=cost(5),
            name="stack",
        )(slot_epoch, epoch_time, rates, band, *given, *carried)
        return keep, send, filtered

    early = list(range(chips - 1))
    *far, early_rows = stack(early, half, half, [windows[x] for x in early])
    keep_far, send_far, late_rows = stack(late, half, half, [windows[x] for x in late], far)
    far = keep_far + swap(send_far.astype(jnp.float16), 1).astype(jnp.float32)
    far = far.astype(jnp.float16)
    far, early_rows = lax.optimization_barrier((far, early_rows))
    other = swap(far, half).astype(jnp.float32) * (1.0 / LINK_SCALE)
    keep_near, send_near, _ = stack(early + late, 0, half, early_rows + late_rows, fresh=False)
    send_near, other = lax.optimization_barrier((send_near.astype(jnp.float16), other))
    near = (keep_near + swap(send_near, 1).astype(jnp.float32)) * (1.0 / LINK_SCALE)
    first = device < half
    near = jnp.where(first, near, other) / jnp.sqrt(jnp.where(first, other, near) + 1.0)
    near = (near * LINK_SCALE).astype(jnp.float16)
    best = jnp.max(near, axis=0)
    best = jnp.maximum(jnp.maximum(best, swap(best, 1)), jnp.maximum(swap(best, half), swap(best, half + 1)))

    pieces = [jnp.concatenate([near[x], best]) for x in range(chips)]
    pieces = [pieces[0]] + [swap(pieces[x], 2 * x) for x in range(1, chips)]
    whole = arrange(pieces, place).astype(jnp.float32) * (1.0 / LINK_SCALE)
    return whole[None, :rows], whole[rows:]


def solution(mesh):
    return jax.shard_map(
        functools.partial(local, mesh.shape["vel"]),
        mesh=mesh,
        in_specs=(P("vel", "groups", None), P("vel", None), P(), P()),
        out_specs=(P("vel", "groups", None), P("groups", None)),
        check_vma=False,
    )
```

```python
import functools

import jax
import jax.numpy as jnp
import ml_dtypes
import numpy as np
from jax import lax
from jax.experimental import pallas as pl
from jax.experimental.pallas import tpu as pltpu
from jax.sharding import PartitionSpec as P

SPLINE = np.array(
    [
        [64.0, 256.0, 64.0, 0.0],
        [27.0, 235.0, 121.0, 1.0],
        [8.0, 184.0, 184.0, 8.0],
        [1.0, 121.0, 235.0, 27.0],
    ],
    np.float32,
)
spline_norm = 147456.0
HALO = 24
LANES = 128
PACK = 16
LINK_SCALE = 64.0


def row_filter(rows):
    band = np.zeros((rows, 4 * LANES), np.float32)
    for row in range(rows):
        for tap in range(4):
            for fraction in range(4):
                band[row, fraction * LANES + (row - tap + 1) % LANES] = SPLINE[fraction, tap]
    return band.astype(ml_dtypes.bfloat16)


def window_kernel(block, image_ref, *refs):
    *window_refs, padded = refs
    place = (lax.axis_index("vel") >> 1) & (len(window_refs) - 1)
    lanes, columns = image_ref.shape
    image = jnp.concatenate([image_ref[...], jnp.zeros((lanes, LANES), image_ref.dtype)], axis=1)
    image = pltpu.roll(image, HALO, 1)
    for first in range(0, columns + LANES, LANES):
        padded[first : first + LANES] = image[:, first : first + LANES].T
    for relative, window_ref in enumerate(window_refs):
        start = pl.multiple_of((place ^ relative) * block, block)
        window_ref[...] = padded[pl.ds(start, block + 2 * HALO)]


def stack_kernel(block, rows, sources, images, first, scale, fresh, carried, slot_ref, time_ref, rate_ref, filter_ref, *refs):
    count = len(sources)
    given, before, refs = refs[:count], refs[count:][:carried], refs[count + carried :]
    keep_ref, send_ref, *refs = refs
    kept, refs = (refs[:count], refs[count:]) if fresh else (given, refs)
    bands, slots, times, rates, semaphores, *bins = refs
    fetches = [
        pltpu.make_async_copy(slot_ref, slots, semaphores.at[0]),
        pltpu.make_async_copy(time_ref, times, semaphores.at[1]),
        pltpu.make_async_copy(rate_ref, rates, semaphores.at[2]),
    ]
    for fetch in fetches:
        fetch.start()
    chips = rates.shape[0] // 8
    together = len(bins)
    turns = bins[0].shape[0] // 4
    reach = bins[0].shape[1] - PACK
    wide = block + 2 * HALO
    lanes = images * rows
    offsets = sorted({rows * number % LANES for number in range(images)})
    if fresh:
        bands[...] = jnp.zeros(bands.shape, bands.dtype)
        for number, offset in enumerate(offsets):
            bands[number, offset : offset + rows] = filter_ref[...]
        for filtered in kept:
            if filtered.shape[2] > wide:
                filtered[:, :, wide:] = jnp.zeros((*filtered.shape[:2], filtered.shape[2] - wide, LANES), filtered.dtype)
    for part in bins:
        part[...] = jnp.zeros(part.shape, part.dtype)
    for index, relative in enumerate(sources):
        filtered, window_ref = kept[index], given[index]
        for number in range(images):
            if fresh:
                low = rows * number // LANES * LANES
                high = min(lanes, (rows * (number + 1) + LANES - 1) // LANES * LANES)
                band = bands[offsets.index(rows * number - low), : high - low]
                product = jnp.dot(window_ref[:, low:high], band, preferred_element_type=jnp.float32)
                product = product.astype(jnp.bfloat16)
                for fraction in range(4):
                    filtered[number, fraction, :wide] = product[:, fraction * LANES : (fraction + 1) * LANES]
            if index == 0 and number == 0:
                for fetch in fetches:
                    fetch.wait()
            source = lax.axis_index("vel") ^ (2 * relative)
            time = times[slots[lax.rem(source * images + number, times.shape[0])]]

            def add(turn, _, time=time, number=number, filtered=filtered):
                for lane in range(together):
                    v = first + turn * together + lane
                    rate = (v >> 1) // chips * 4 * chips + (v & 1) * 2 * chips + (v >> 1) % chips * 2
                    row_offset = (rates[rate] * time) >> 5
                    column_offset = (rates[rate + 1] * time) >> 5
                    start = HALO - 1 + (column_offset >> 2)
                    even = pl.multiple_of((start >> 4) << 4, PACK)
                    shifted = filtered[number, row_offset & 3, pl.ds(even, reach), :]
                    shifted = pltpu.roll(shifted, (LANES - (row_offset >> 2)) & (LANES - 1), 1)
                    place = 4 * turn + (column_offset & 3)
                    bins[lane][place, pl.ds(PACK - (start - even), reach), :] += shifted.astype(jnp.float32)
                return _

            if turns == 1:
                add(0, 0)
            else:
                lax.fori_loop(0, turns, add, 0)

    def finish(turn, _):
        for lane in range(together):
            v = turn * together + lane
            total = jnp.zeros((block, LANES), jnp.float32)
            for fraction in range(4):
                for tap in range(4):
                    if SPLINE[fraction, tap]:
                        taken = bins[lane][4 * turn + fraction, PACK + tap : PACK + tap + block, :]
                        total = total + float(SPLINE[fraction, tap]) * taken
            total = (total * scale).T[:rows]
            if before:
                total = total + before[lane & 1][v >> 1]
            (send_ref if lane & 1 else keep_ref)[v >> 1] = total
        return _

    if turns == 1:
        finish(0, 0)
    else:
        lax.fori_loop(0, turns, finish, 0)


def arrange(pieces, place):
    step = 1
    while step < len(pieces):
        flip = (place & step) != 0
        pieces = [jnp.where(flip, pieces[x ^ step], pieces[x]) for x in range(len(pieces))]
        step *= 2
    return jnp.concatenate(pieces, axis=-1)


def local(axis_size, epoch_maps, velocity, slot_epoch, epoch_time):
    per_device, rows, columns = epoch_maps.shape
    half = axis_size // 2
    chips = half // 2
    block = columns // chips
    device = lax.axis_index("vel").astype(jnp.int32)
    place = device % half // 2

    def swap(array, bits):
        return lax.ppermute(array, "vel", [(i, i ^ bits) for i in range(axis_size)])

    smem = pl.BlockSpec(memory_space=pltpu.SMEM)
    vmem = pl.BlockSpec(memory_space=pltpu.VMEM)
    hbm = pl.BlockSpec(memory_space=pltpu.HBM)
    lanes = per_device * rows
    wide = block + 2 * HALO
    shape = jax.ShapeDtypeStruct

    def cost(microseconds):
        return pl.CostEstimate(flops=microseconds * 10**9, bytes_accessed=microseconds * 3 * 10**6, transcendentals=0)


    rates = velocity.reshape(-1)
    rates = jnp.concatenate([rates] + [swap(rates, 2 * x) for x in range(1, chips)])
    windows = list(pl.pallas_call(
        functools.partial(window_kernel, block),
        out_shape=[shape((wide, lanes), epoch_maps.dtype)] * chips,
        in_specs=[vmem],
        out_specs=[vmem] * chips,
        scratch_shapes=[pltpu.VMEM((columns + LANES, lanes), epoch_maps.dtype)],
        compiler_params=pltpu.CompilerParams(vmem_limit_bytes=56 * 1024 * 1024),
        cost_estimate=cost(3),
        name="windows",
    )(epoch_maps.reshape(lanes, columns)))
    late = [chips - 1]
    windows[2:], rates = lax.optimization_barrier((windows[2:], rates))
    rates = jnp.concatenate([rates, swap(rates, 1)])
    rates = jnp.concatenate([rates, swap(rates, half)])
    windows = [windows[0]] + [swap(windows[x], 2 * x) for x in range(1, chips)]

    reach = (block + 2 + PACK + PACK - 1) // PACK * PACK
    band = jnp.asarray(row_filter(rows))

    tall = max(wide, 2 * PACK + reach)

    def stack(sources, first, count, given, carried=(), fresh=True):
        together = min(count, 16)
        filtered = shape((per_device, 4, tall, LANES), jnp.bfloat16)
        keep, send, *filtered = pl.pallas_call(
            functools.partial(
                stack_kernel,
                *(block, rows, sources, per_device, first, LINK_SCALE / spline_norm, fresh, len(carried)),
            ),
            out_shape=[shape((count // 2, rows, block), jnp.float32)] * 2 + [filtered] * (fresh * len(sources)),
            in_specs=[hbm, hbm, hbm, vmem]
            + [vmem] * (len(sources) + len(carried)),
            out_specs=[vmem] * (2 + fresh * len(sources)),
            scratch_shapes=[
                pltpu.VMEM((4, 2 * LANES, 4 * LANES), jnp.bfloat16),
                pltpu.SMEM(slot_epoch.shape, jnp.int32),
                pltpu.SMEM(epoch_time.shape, jnp.int32),
                pltpu.SMEM(rates.shape, jnp.int32),
                pltpu.SemaphoreType.DMA((3,)),
            ]
            + [pltpu.VMEM((4 * count // together, reach + PACK, LANES), jnp.float32)] * together,
            compiler_params=pltpu.CompilerParams(vmem_limit_bytes=32 * 1024 * 1024),
            cost_estimate=cost(5),
            name="stack",
        )(slot_epoch, epoch_time, rates, band, *given, *carried)
        return keep, send, filtered

    early = list(range(chips - 1))
    *far, early_rows = stack(early, half, half, [windows[x] for x in early])
    keep_far, send_far, late_rows = stack(late, half, half, [windows[x] for x in late], far)
    far = keep_far + swap(send_far.astype(jnp.float16), 1).astype(jnp.float32)
    far = far.astype(jnp.float16)
    far, early_rows = lax.optimization_barrier((far, early_rows))
    other = swap(far, half).astype(jnp.float32) * (1.0 / LINK_SCALE)
    keep_near, send_near, _ = stack(early + late, 0, half, early_rows + late_rows, fresh=False)
    send_near, other = lax.optimization_barrier((send_near.astype(jnp.float16), other))
    near = (keep_near + swap(send_near, 1).astype(jnp.float32)) * (1.0 / LINK_SCALE)
    first = device < half
    near = jnp.where(first, near, other) / jnp.sqrt(jnp.where(first, other, near) + 1.0)
    near = (near * LINK_SCALE).astype(jnp.float16)
    best = jnp.max(near, axis=0)
    best = jnp.maximum(jnp.maximum(best, swap(best, 1)), jnp.maximum(swap(best, half), swap(best, half + 1)))

    pieces = [jnp.concatenate([near[x], best]) for x in range(chips)]
    pieces = [pieces[0]] + [swap(pieces[x], 2 * x) for x in range(1, chips)]
    whole = arrange(pieces, place).astype(jnp.float32) * (1.0 / LINK_SCALE)
    return whole[None, :rows], whole[rows:]


def solution(mesh):
    return jax.shard_map(
        functools.partial(local, mesh.shape["vel"]),
        mesh=mesh,
        in_specs=(P("vel", "groups", None), P("vel", None), P(), P()),
        out_specs=(P("vel", "groups", None), P("groups", None)),
        check_vma=False,
    )
```
